512 devices in a mesh: dp: 32 (over x_lo, z, core), seq: 16 (over x_hi, y).
Axes of the slice: x: 4 (x_hi: 2, x_lo: 2; x = x_hi * 2 + x_lo), y: 8, z: 8, core: 2. Of those that a mesh axis runs over, the one named last changes fastest.
Arguments:
- queries: bfloat16 [32, 2048, 2048], P('dp', 'seq'), may hold values from -80 to 80
- keys: bfloat16 [32, 2048, 2048], P('dp', 'seq'), may hold values from -5 to 5
- values: bfloat16 [32, 2048, 2048], P('dp', 'seq'), may hold values from -6 to 6
- grads_out: bfloat16 [32, 2048, 2048], P('dp', 'seq'), may hold values from -6 to 6
- q_scale: float32 [16, 128], replicated, may hold values from 0.5 to 2
- lengths: int32 [32], P('dp'), may hold values from 1 to 2048, 32768 in all
Outputs:
- attention_out: bfloat16 [32, 2048, 2048], P('dp', 'seq')
- query_grad: bfloat16 [32, 2048, 2048], P('dp', 'seq')
- key_grad: bfloat16 [32, 2048, 2048], P('dp', 'seq')
- value_grad: bfloat16 [32, 2048, 2048], P('dp', 'seq')
- scale_grad: float32 [16, 128], replicated
The draws below stay inside these ranges and needn't reach their ends.
Inputs may be any that keep to these rules, and one draw needn't show every extreme that they name: `lengths`: the valid tokens of a mesh are its first ones; some mesh has all 2048 valid.
All inputs are finite; a program needn't handle non-finite values. No bound on the sum of `lengths` on one device may be relied on, other than what follows from the above.
Results may differ from the reference program's by a relative error of at most 0.007.
Values may be sent and summed in bfloat16 or wider, within the bound.
No kernel may reach another device: no remote copies, remote signals or barrier semaphores. Data moves between devices by JAX's collectives and lax.ppermute only.
A program may use at most 64 MiB of HBM per device.

```python
import math
import jax
import jax.numpy as jnp
import numpy as np
from jax import lax

H = 16
HD = 128
D = 2048
TOKENS_MESH = 2048
MESHES = 32


def shared_keys(key):
    return jnp.clip(jax.random.normal(key, (MESHES, TOKENS_MESH, D), jnp.float32), -4.0, 4.0)


def draw_keys(key, part):
    base = shared_keys(key)
    return base.astype(jnp.bfloat16)


def draw_queries(key, part):
    key = jax.random.fold_in(key, 7)
    fresh = jnp.clip(jax.random.normal(key, (MESHES, TOKENS_MESH, D), jnp.float32), -4.0, 4.0)
    return fresh.astype(jnp.bfloat16)


def block_levels(key, shape, shards, low, top_value):
    def one(dim, parts):
        draws = jax.random.uniform(jax.random.fold_in(jax.random.fold_in(key, 6), dim), (parts,), jnp.float32, low / len(shards), top_value / len(shards))
        return jnp.repeat(jnp.exp(draws), shape[dim] // parts).reshape((-1,) + (1,) * (len(shape) - dim - 1))

    level = one(*shards[0])
    for cut in shards[1:]:
        level = level * one(*cut)
    return level


def profile(amount, total, limit, skew):
    loads = [(1 << 20) // math.isqrt(standing ** skew) + 1 for standing in range(2, amount + 1)]
    rest, given = total - limit - (amount - 1), [1] * (amount - 1)
    while rest > 0:
        candidates = [i for i in range(amount - 1) if given[i] < limit]
        mass, remaining = sum([loads[i] for i in candidates]), rest
        for i in candidates:
            addition = min(limit - given[i], max(1, remaining * loads[i] // mass), rest)
            given[i] = given[i] + addition
            rest = rest - addition
    return np.array([limit] + given)


def ragged_sizes(own_key, amount, total, most, skew):
    if amount == 2:
        one = jax.random.randint(own_key, (), max(1, total - most), min(most, total - 1) + 1)
        return jnp.stack([one, total - one])
    sizes = jnp.asarray(profile(amount, total, most, skew), jnp.int32)
    twos = (amount - 1) // 2
    donor, receiver = sizes[1:1 + 2 * twos:2], sizes[2:2 + 2 * twos:2]
    margin = jnp.minimum(donor - 1, most - receiver)
    shifted = jax.random.randint(jax.random.fold_in(own_key, 1), (twos,), 0, 1 << 20) % (margin + 1)
    sizes = sizes.at[1:1 + 2 * twos:2].set(donor - shifted).at[2:2 + 2 * twos:2].set(receiver + shifted)
    return sizes[jax.random.permutation(jax.random.fold_in(own_key, 2), amount)]


def bell_draw(key, shape, scale, reach, split=(), kind=jnp.bfloat16):
    entries = scale * jax.random.normal(key, shape, jnp.float32)
    if split:
        entries = entries * block_levels(key, shape, split, -0.22, 0.18)
    return jnp.clip(entries, -reach, reach).astype(kind)


def setup_inputs(seed: int = 0) -> dict:
    streams_of = jax.random.split(jax.random.key(seed), 7)
    return {
        "queries": draw_queries(jax.random.fold_in(streams_of[6], 71), 0),
        "keys": draw_keys(jax.random.fold_in(streams_of[6], 71), 0),
        "values": bell_draw(streams_of[2], (MESHES, TOKENS_MESH, D), 1.0, 6.0, ((0, 32), (1, 16))),
        "grads_out": bell_draw(streams_of[3], (MESHES, TOKENS_MESH, D), 1.0, 6.0, ((0, 32), (1, 16))),
        "q_scale": jnp.clip(jnp.exp(jax.random.uniform(streams_of[4], (H, HD), jnp.float32, math.log(0.5), math.log(2.0))), 0.5, 2.0),
        "lengths": ragged_sizes(streams_of[5], MESHES, MESHES * TOKENS_MESH // 2, TOKENS_MESH, 2).astype(jnp.int32),
    }


NEG = -1e+30

def reference(queries, keys, values, grads_out, q_scale, lengths):
    inverse = 1.0 / math.sqrt(HD)
    scale_row = q_scale.reshape(1, D)
    positions = jnp.arange(TOKENS_MESH, dtype=jnp.int32)
    highest = lax.Precision.HIGHEST

    def one_mesh(items):
        mesh_queries, mesh_keys, mesh_values, mesh_grads, mesh_length = items
        valid = positions < mesh_length
        valid_row = valid.astype(jnp.float32)
        scaled = (mesh_queries.astype(jnp.float32) * scale_row).astype(jnp.bfloat16)
        scaled = lax.optimization_barrier(scaled)
        head_q = scaled.astype(jnp.float32).reshape(TOKENS_MESH, H, HD)
        head_k = mesh_keys.astype(jnp.float32).reshape(TOKENS_MESH, H, HD)
        head_v = mesh_values.astype(jnp.float32).reshape(TOKENS_MESH, H, HD)
        masked = (mesh_grads.astype(jnp.float32) * valid_row[:, None]).reshape(TOKENS_MESH, H, HD)
        raw = jnp.einsum('qhd,khd->hqk', head_q, head_k, precision=highest) * inverse
        scores = jnp.where(valid[None, None, :], raw, NEG)
        top = lax.optimization_barrier(jnp.max(scores, axis=2, keepdims=True))
        expo = jnp.exp(scores - top)
        probs = expo / lax.optimization_barrier(jnp.sum(expo, axis=2, keepdims=True))
        probs_b = lax.optimization_barrier(probs.astype(jnp.bfloat16)).astype(jnp.float32)
        attended = jnp.einsum('hqk,khd->qhd', probs_b, head_v, precision=highest) * valid_row[:, None, None]
        dprob = jnp.einsum('qhd,khd->hqk', masked, head_v, precision=highest)
        delta = lax.optimization_barrier(jnp.sum(probs * dprob, axis=2, keepdims=True))
        dscore = lax.optimization_barrier((probs * (dprob - delta)).astype(jnp.bfloat16)).astype(jnp.float32)
        dvalues = jnp.einsum('hqk,qhd->khd', probs_b, masked, precision=highest)
        dscaled = (jnp.einsum('hqk,khd->qhd', dscore, head_k, precision=highest) * inverse).astype(jnp.bfloat16)
        dscaled = lax.optimization_barrier(dscaled)
        dkeys = jnp.einsum('hqk,qhd->khd', dscore, head_q, precision=highest) * inverse
        dscaled_flat = dscaled.reshape(TOKENS_MESH, D).astype(jnp.float32)
        query_grad = (dscaled_flat * scale_row).astype(jnp.bfloat16)
        scale_term = lax.optimization_barrier(jnp.sum(dscaled_flat * mesh_queries.astype(jnp.float32), axis=0))
        return (attended.astype(jnp.bfloat16).reshape(TOKENS_MESH, D), query_grad, dkeys.astype(jnp.bfloat16).reshape(TOKENS_MESH, D), dvalues.astype(jnp.bfloat16).reshape(TOKENS_MESH, D), scale_term)
    results = lax.map(one_mesh, (queries, keys, values, grads_out, lengths))
    scale_grad = lax.optimization_barrier(jnp.sum(results[4], axis=0)).reshape(H, HD)
    return (results[0], results[1], results[2], results[3], scale_grad)
```

```python
import functools
import math

import jax
import jax.numpy as jnp
from jax import lax
from jax.experimental import pallas as pl
from jax.experimental.pallas import tpu as pltpu
from jax.sharding import Mesh, PartitionSpec as P

f32 = jnp.float32
bf16 = jnp.bfloat16
NEG = -1e30
BLOCK_Q = 512
BLOCK_K = 1024
ALONG_ROWS = (((1,), (1,)), ((), ()))
PLAIN = (((1,), (0,)), ((), ()))
VMEM = pl.BlockSpec(memory_space=pltpu.VMEM)
SMEM = pl.BlockSpec(memory_space=pltpu.SMEM)


def dot(a, b, dims=PLAIN):
    return lax.dot_general(a, b, dims, preferred_element_type=f32)


def split_kernel(heads, size, *refs):
    sources, out_ref = refs[:-1], refs[-1]
    for head in range(heads):
        for place, source in enumerate(sources):
            out_ref[head, place] = source[:, head * size : (head + 1) * size]


def join_kernel(heads, size, *refs):
    source, outs = refs[0], refs[1:]
    for head in range(heads):
        for place, out in enumerate(outs):
            out[:, head * size : (head + 1) * size] = source[head, place]


def attention_kernel(
    tokens, block_q, block_k, length_ref, scale_ref, x_ref, out_ref, term_ref,
    keys_t, values_t, scores, dprobs, dkeys, dvalues,
):
    part, size = x_ref.shape[2], x_ref.shape[3]
    inverse = 1.0 / math.sqrt(size)
    factor = inverse * math.log2(math.e)
    length = length_ref[0]
    q_blocks = (length + block_q - 1) // block_q
    k_blocks = (length + block_k - 1) // block_k
    q_parts, k_parts = block_q // part, block_k // part
    scale = scale_ref[...]

    def rows_of(block, parts, operand):
        return x_ref[pl.ds(block * parts, parts), operand].reshape(parts * part, size)

    def key_rows(block):
        return pl.ds(pl.multiple_of(block * block_k, block_k), block_k)

    def fold(wide, op):
        return op(wide.reshape(block_k // 8, 8, block_q), axis=0)

    def transpose(block, carry):
        keys_t[:, key_rows(block)] = rows_of(block, k_parts, 1).T
        values_t[:, key_rows(block)] = rows_of(block, k_parts, 2).T
        return carry

    lax.fori_loop(0, k_blocks, transpose, 0)
    term_ref[...] = jnp.zeros_like(term_ref)
    dkeys[...] = jnp.zeros_like(dkeys)
    dvalues[...] = jnp.zeros_like(dvalues)

    def query_block(block, carry):
        positions = lax.broadcasted_iota(jnp.int32, (block_q, size), 0) + block * block_q
        valid = positions < length
        queries = rows_of(block, q_parts, 0).astype(f32)
        scaled = (queries * scale).astype(bf16)
        grads = jnp.where(valid, rows_of(block, q_parts, 3).astype(f32), 0.0).astype(bf16)

        def score_step(j, top):
            raw = dot(rows_of(j, k_parts, 1), scaled, ALONG_ROWS)
            places = lax.broadcasted_iota(jnp.int32, (block_k, block_q), 0) + j * block_k
            raw = jnp.where(places < length, raw, NEG)
            scores[key_rows(j), :] = raw
            return jnp.maximum(top, fold(raw, jnp.max))

        top = lax.fori_loop(0, k_blocks, score_step, jnp.full((8, block_q), NEG, f32))
        top = jnp.max(top, axis=0, keepdims=True)

        def prob_step(j, sums):
            total, weighted = sums
            dprob = dot(rows_of(j, k_parts, 2), grads, ALONG_ROWS)
            expo = jnp.exp2((scores[key_rows(j), :] - top) * factor)
            scores[key_rows(j), :] = expo
            dprobs[key_rows(j), :] = dprob
            return total + fold(expo, jnp.sum), weighted + fold(expo * dprob, jnp.sum)

        zero = jnp.zeros((8, block_q), f32)
        total, weighted = lax.fori_loop(0, k_blocks, prob_step, (zero, zero))
        share = 1.0 / jnp.sum(total, axis=0, keepdims=True)
        delta = jnp.sum(weighted, axis=0, keepdims=True) * share

        def grad_step(j, sums):
            out_t, dscaled_t = sums
            rows = key_rows(j)
            probs = scores[rows, :] * share
            probs_b = probs.astype(bf16)
            dscore = (probs * (dprobs[rows, :] - delta)).astype(bf16)
            dvalues[rows, :] += dot(probs_b, grads)
            dkeys[rows, :] += dot(dscore, scaled)
            return out_t + dot(values_t[:, rows], probs_b), dscaled_t + dot(keys_t[:, rows], dscore)

        zero = jnp.zeros((size, block_q), f32)
        out_t, dscaled_t = lax.fori_loop(0, k_blocks, grad_step, (zero, zero))
        attended = jnp.where(valid, out_t.T, 0.0).astype(bf16)
        dscaled = (dscaled_t.T * inverse).astype(bf16).astype(f32)
        term_ref[...] += jnp.sum((dscaled * queries).reshape(block_q // 8, 8, size), axis=0)
        here = pl.ds(block * q_parts, q_parts)
        out_ref[here, 0] = attended.reshape(q_parts, part, size)
        out_ref[here, 1] = (dscaled * scale).astype(bf16).reshape(q_parts, part, size)
        return carry

    lax.fori_loop(0, q_blocks, query_block, 0)

    def clear(block, carry):
        out_ref[pl.ds(block * q_parts, q_parts), 0:2] = jnp.zeros((q_parts, 2, part, size), bf16)
        return carry

    lax.fori_loop(q_blocks, tokens // block_q, clear, 0)

    def finish(j, carry):
        here, rows = pl.ds(j * k_parts, k_parts), key_rows(j)
        out_ref[here, 2] = (dkeys[rows, :] * inverse).astype(bf16).reshape(k_parts, part, size)
        out_ref[here, 3] = dvalues[rows, :].astype(bf16).reshape(k_parts, part, size)
        return carry

    lax.fori_loop(0, tokens // block_k, finish, 0)


def attend(length, scale, x):
    blocks, _, part, size = x.shape
    tokens = blocks * part
    block_q, block_k = min(BLOCK_Q, tokens), min(BLOCK_K, tokens)
    flops = 12 * tokens * tokens * size
    return pl.pallas_call(
        functools.partial(attention_kernel, tokens, block_q, block_k),
        out_shape=(
            jax.ShapeDtypeStruct(x.shape, bf16),
            jax.ShapeDtypeStruct((8, size), f32),
        ),
        in_specs=[SMEM, VMEM, VMEM],
        out_specs=(VMEM, VMEM),
        scratch_shapes=[
            pltpu.VMEM((size, tokens), bf16),
            pltpu.VMEM((size, tokens), bf16),
            pltpu.VMEM((tokens, block_q), f32),
            pltpu.VMEM((tokens, block_q), f32),
            pltpu.VMEM((tokens, size), f32),
            pltpu.VMEM((tokens, size), f32),
        ],
        cost_estimate=pl.CostEstimate(
            flops=flops, bytes_accessed=4 * x.size, transcendentals=tokens * tokens
        ),
        compiler_params=pltpu.CompilerParams(vmem_limit_bytes=40 * 1024 * 1024),
        name="attention",
    )(length, scale, x)


def swap_sum(value, axis, step):
    count = lax.axis_size(axis)
    return value + lax.ppermute(value, axis, [(i, i ^ step) for i in range(count)])


def per_device(queries, keys, values, grads_out, q_scale, lengths):
    heads, size = q_scale.shape
    local, width = queries.shape[1:]
    seq = ("xh", "y")
    me = lax.axis_index(seq)
    small = pltpu.CompilerParams(vmem_limit_bytes=16 * 1024 * 1024)
    x = pl.pallas_call(
        functools.partial(split_kernel, heads, size),
        out_shape=jax.ShapeDtypeStruct((heads, 4, local, size), bf16),
        in_specs=[VMEM] * 4,
        out_specs=VMEM,
        compiler_params=small,
        name="split",
    )(queries[0], keys[0], values[0], grads_out[0])
    x = lax.all_to_all(x, seq, 0, 0, tiled=True)
    scale = lax.dynamic_slice_in_dim(q_scale, me, 1, 0)
    results, term = attend(lengths, scale, x)
    back = lax.all_to_all(results, seq, 0, 0, tiled=True)

    term = jnp.sum(term, axis=0, keepdims=True)
    for axis, step in (("c", 1), ("xl", 1), ("z", 1), ("z", 2), ("z", 4)):
        term = swap_sum(term, axis, step)
    grid = jnp.where(lax.broadcasted_iota(jnp.int32, (heads, size), 0) == me, term, 0.0)
    for axis, step in (("xh", 1), ("y", 1), ("y", 2), ("y", 4)):
        grid = swap_sum(grid, axis, step)

    outs = pl.pallas_call(
        functools.partial(join_kernel, heads, size),
        out_shape=[jax.ShapeDtypeStruct((local, width), bf16)] * 4,
        in_specs=[VMEM],
        out_specs=[VMEM] * 4,
        compiler_params=small,
        name="join",
    )(back)
    return tuple(out[None] for out in outs) + (grid,)


def solution(mesh):
    fine = Mesh(mesh.devices.reshape(2, 8, 2, 2, 8), ("xl", "z", "c", "xh", "y"))
    tokens = P(("xl", "z", "c"), ("xh", "y"), None)
    return jax.shard_map(
        per_device,
        mesh=fine,
        in_specs=(tokens, tokens, tokens, tokens, P(), P(("xl", "z", "c"))),
        out_specs=(tokens, tokens, tokens, tokens, P()),
        check_vma=False,
    )
```

```python
import functools
import math

import jax
import jax.numpy as jnp
from jax import lax
from jax.experimental import pallas as pl
from jax.experimental.pallas import tpu as pltpu
from jax.sharding import Mesh, PartitionSpec as P

f32 = jnp.float32
bf16 = jnp.bfloat16
NEG = -1e30
BLOCK_Q = 512
ALONG_ROWS = (((1,), (1,)), ((), ()))
PLAIN = (((1,), (0,)), ((), ()))
VMEM = pl.BlockSpec(memory_space=pltpu.VMEM)
HBM = pl.BlockSpec(memory_space=pltpu.HBM)
SMEM = pl.BlockSpec(memory_space=pltpu.SMEM)


def dot(a, b, dims=PLAIN):
    return lax.dot_general(a, b, dims, preferred_element_type=f32)


def split_kernel(heads, size, *refs):
    sources, out_ref, staged, arrived = refs[:4], refs[4], refs[5], refs[6]
    steps = arrived.shape[1]
    rows = staged.shape[1] // steps

    def fetch(place, step):
        here = pl.ds(step * rows, rows)
        return pltpu.make_async_copy(
            sources[place].at[here], staged.at[place, here], arrived.at[place, step]
        )

    for step in range(steps):
        for place in range(4):
            fetch(place, step).start()
    for step in range(steps):
        here = pl.ds(step * rows, rows)
        for place in range(4):
            fetch(place, step).wait()
            for head in range(heads):
                out_ref[head, place, here] = staged[place, here, head * size : (head + 1) * size]


def join_kernel(heads, size, *refs):
    source, outs, staged, sent = refs[0], refs[1:5], refs[5], refs[6]
    steps = sent.shape[1]
    rows = staged.shape[1] // steps

    def store(place, step):
        here = pl.ds(step * rows, rows)
        return pltpu.make_async_copy(
            staged.at[place, here], outs[place].at[here], sent.at[place, step]
        )

    for step in range(steps):
        here = pl.ds(step * rows, rows)
        for place in range(4):
            for head in range(heads):
                staged[place, here, head * size : (head + 1) * size] = source[head, place, here]
            store(place, step).start()
    for step in range(steps):
        for place in range(4):
            store(place, step).wait()


def attention_kernel(block_q, length_ref, scale_ref, x_ref, out_ref, term_ref, *scratch):
    tokens = x_ref.shape[0] * x_ref.shape[2]
    length = length_ref[0]
    half = tokens // 2

    @pl.when(length <= half)
    def _():
        attend_keys(half, block_q, length, scale_ref, x_ref, out_ref, term_ref, *scratch)

    @pl.when(length > half)
    def _():
        attend_keys(tokens, block_q, length, scale_ref, x_ref, out_ref, term_ref, *scratch)


def attend_keys(
    width, block_q, length, scale_ref, x_ref, out_ref, term_ref,
    keys_t, values_t, scaled_ref, grads_ref, scores, expos, dprobs, dkeys, dvalues, sent_q, sent_k, results,
):
    blocks, operands, part, size = x_ref.shape
    tokens = blocks * part
    inverse = 1.0 / math.sqrt(size)
    factor = inverse * math.log2(math.e)
    q_blocks = (length + block_q - 1) // block_q
    q_parts, k_parts = block_q // part, width // part
    scale = scale_ref[...]
    rows = pl.ds(0, width)

    def rows_of(block, parts, operand):
        return x_ref[pl.ds(block * parts, parts), operand].reshape(parts * part, size)

    def query_rows(block):
        return pl.ds(pl.multiple_of(block * block_q, block_q), block_q)

    def fold(wide, op):
        return op(op(wide.reshape(width // 8, 8, block_q), axis=0), axis=0, keepdims=True)

    def valid_rows(block):
        return lax.broadcasted_iota(jnp.int32, (block_q, size), 0) + block * block_q < length

    def send_queries(block):
        here = pl.ds(block * q_parts, q_parts)
        return pltpu.make_async_copy(
            results.at[here, 0:2], out_ref.at[here, 0:2], sent_q.at[block]
        )

    def send_keys(block):
        here = pl.ds(block * q_parts, q_parts)
        return pltpu.make_async_copy(
            results.at[here, 2:4], out_ref.at[here, 2:4], sent_k.at[block]
        )

    def prepare_queries(block, carry):
        here = query_rows(block)
        scaled_ref[here, :] = (rows_of(block, q_parts, 0).astype(f32) * scale).astype(bf16)
        grads = rows_of(block, q_parts, 3).astype(f32)
        grads_ref[here, :] = jnp.where(valid_rows(block), grads, 0.0).astype(bf16)
        return carry

    def sweep(third=None, second=None, first=None):
        results_of = ()
        if third:
            block_c, share, delta = third
            scaled_c, grads_c = scaled_ref[query_rows(block_c), :], grads_ref[query_rows(block_c), :]
            probs = expos[rows, :] * share
            probs_b = probs.astype(bf16)
            dscore = (probs * (dprobs[rows, :] - delta)).astype(bf16)
            dvalues[rows, :] += dot(probs_b, grads_c)
            dkeys[rows, :] += dot(dscore, scaled_c)
            results_of += (dot(values_t[:, rows], probs_b), dot(keys_t[:, rows], dscore))
        if second:
            block_b, top = second
            dprob = dot(rows_of(0, k_parts, 2), grads_ref[query_rows(block_b), :], ALONG_ROWS)
            expo = jnp.exp2((scores[rows, :] - top) * factor)
            expos[rows, :] = expo
            dprobs[rows, :] = dprob
            share = 1.0 / fold(expo, jnp.sum)
            results_of += (share, fold(expo * dprob, jnp.sum) * share)
        if first is not None:
            raw = dot(rows_of(0, k_parts, 1), scaled_ref[query_rows(first), :], ALONG_ROWS)
            places = lax.broadcasted_iota(jnp.int32, (width, block_q), 0)
            raw = jnp.where(places < length, raw, NEG)
            scores[rows, :] = raw
            results_of += (fold(raw, jnp.max),)
        return results_of

    def finish_block(block, out_t, dscaled_t):
        attended = jnp.where(valid_rows(block), out_t.T, 0.0).astype(bf16)
        dscaled = (dscaled_t.T * inverse).astype(bf16).astype(f32)
        queries = rows_of(block, q_parts, 0).astype(f32)
        term_ref[...] += jnp.sum((dscaled * queries).reshape(block_q // 8, 8, size), axis=0)
        here = pl.ds(block * q_parts, q_parts)
        results[here, 0] = attended.reshape(q_parts, part, size)
        results[here, 1] = (dscaled * scale).astype(bf16).reshape(q_parts, part, size)
        send_queries(block).start()

    lax.fori_loop(0, q_blocks, prepare_queries, 0)
    last = q_blocks - 1
    (top,) = sweep(first=0)
    for start in range(0, width, 512):
        span = min(512, width - start)
        here = pl.ds(start, span)
        keys_t[:, here] = rows_of(start // span, span // part, 1).T
        values_t[:, here] = rows_of(start // span, span // part, 2).T
    term_ref[...] = jnp.zeros_like(term_ref)
    dkeys[rows, :] = jnp.zeros((width, size), f32)
    dvalues[rows, :] = jnp.zeros((width, size), f32)
    share, delta, top = sweep(second=(0, top), first=jnp.minimum(1, last))

    def query_block(block, carry):
        share, delta, top = carry
        after = jnp.minimum(block + 1, last)
        out_t, dscaled_t, *carry = sweep((block, share, delta), (after, top), jnp.minimum(block + 2, last))
        finish_block(block, out_t, dscaled_t)
        return tuple(carry)

    share, delta, top = lax.fori_loop(0, last, query_block, (share, delta, top))
    finish_block(last, *sweep((last, share, delta)))

    def clear_queries(block, carry):
        results[pl.ds(block * q_parts, q_parts), 0:2] = jnp.zeros((q_parts, 2, part, size), bf16)
        send_queries(block).start()
        return carry

    lax.fori_loop(q_blocks, tokens // block_q, clear_queries, 0)
    for block in range(tokens // block_q):
        here, mine = pl.ds(block * q_parts, q_parts), pl.ds(block * block_q, block_q)
        if block * block_q < width:
            results[here, 2] = (dkeys[mine, :] * inverse).astype(bf16).reshape(q_parts, part, size)
            results[here, 3] = dvalues[mine, :].astype(bf16).reshape(q_parts, part, size)
        else:
            results[here, 2:4] = jnp.zeros((q_parts, 2, part, size), bf16)
        send_keys(block).start()
    for block in range(tokens // block_q):
        send_queries(block).wait()
        send_keys(block).wait()


def attend(length, scale, x):
    blocks, _, part, size = x.shape
    tokens = blocks * part
    block_q = min(BLOCK_Q, tokens)
    copies = tokens // block_q
    return pl.pallas_call(
        functools.partial(attention_kernel, block_q),
        out_shape=(jax.ShapeDtypeStruct(x.shape, bf16), jax.ShapeDtypeStruct((8, size), f32)),
        in_specs=[SMEM, VMEM, VMEM],
        out_specs=(HBM, VMEM),
        scratch_shapes=[pltpu.VMEM((size, tokens), bf16)] * 2
        + [pltpu.VMEM((tokens, size), bf16)] * 2
        + [pltpu.VMEM((tokens, block_q), f32)] * 3
        + [pltpu.VMEM((tokens, size), f32)] * 2
        + [pltpu.SemaphoreType.DMA((copies,))] * 2
        + [pltpu.VMEM(x.shape, bf16)],
        cost_estimate=pl.CostEstimate(
            flops=12 * tokens * tokens * size, bytes_accessed=4 * x.size, transcendentals=tokens * tokens
        ),
        compiler_params=pltpu.CompilerParams(vmem_limit_bytes=48 * 1024 * 1024),
        name="attention",
    )(length, scale, x)


def per_device(queries, keys, values, grads_out, q_scale, lengths):
    heads, size = q_scale.shape
    local, width = queries.shape[1:]
    seq = ("xh", "y")
    me = lax.axis_index(seq)
    small = pltpu.CompilerParams(vmem_limit_bytes=16 * 1024 * 1024)
    steps = max(local // 32, 1)
    x = pl.pallas_call(
        functools.partial(split_kernel, heads, size),
        out_shape=jax.ShapeDtypeStruct((heads, 4, local, size), bf16),
        in_specs=[HBM] * 4,
        out_specs=VMEM,
        scratch_shapes=[
            pltpu.VMEM((4, local, width), bf16),
            pltpu.SemaphoreType.DMA((4, steps)),
        ],
        compiler_params=pltpu.CompilerParams(vmem_limit_bytes=56 * 1024 * 1024),
        name="split",
    )(queries[0], keys[0], values[0], grads_out[0])
    x = lax.all_to_all(x, seq, 0, 0, tiled=True)
    scale = lax.dynamic_slice_in_dim(q_scale, me, 1, 0)
    results, term = attend(lengths, scale, x)
    back = lax.all_to_all(results, seq, 0, 0, tiled=True)

    term = jnp.sum(term, axis=0, keepdims=True)
    across = lax.ppermute(term, "xh", [(0, 1), (1, 0)])
    own = lax.broadcasted_iota(jnp.int32, (2, size), 0) == lax.axis_index("xh")
    pair = jnp.where(own, term, across)
    for axis in ("c", "xl", "z"):
        pair = lax.psum(pair, axis)
    grid = lax.all_gather(pair, "y", axis=1).reshape(heads, size)

    outs = pl.pallas_call(
        functools.partial(join_kernel, heads, size),
        out_shape=[jax.ShapeDtypeStruct((local, width), bf16)] * 4,
        in_specs=[VMEM],
        out_specs=[HBM] * 4,
        scratch_shapes=[
            pltpu.VMEM((4, local, width), bf16),
            pltpu.SemaphoreType.DMA((4, steps)),
        ],
        compiler_params=small,
        name="join",
    )(back)
    return tuple(out[None] for out in outs) + (grid,)


def solution(mesh):
    fine = Mesh(mesh.devices.reshape(2, 8, 2, 2, 8), ("xl", "z", "c", "xh", "y"))
    tokens = P(("xl", "z", "c"), ("xh", "y"), None)
    return jax.shard_map(
        per_device,
        mesh=fine,
        in_specs=(tokens, tokens, tokens, tokens, P(), P(("xl", "z", "c"))),
        out_specs=(tokens, tokens, tokens, tokens, P()),
        check_vma=False,
    )
```

```python
import functools
import math

import jax
import jax.numpy as jnp
from jax import lax
from jax.experimental import pallas as pl
from jax.experimental.pallas import tpu as pltpu
from jax.sharding import Mesh, PartitionSpec as P

f32 = jnp.float32
bf16 = jnp.bfloat16
NEG = -1e30
BLOCK_Q = 512
ALONG_ROWS = (((1,), (1,)), ((), ()))
PLAIN = (((1,), (0,)), ((), ()))
VMEM = pl.BlockSpec(memory_space=pltpu.VMEM)
HBM = pl.BlockSpec(memory_space=pltpu.HBM)
SMEM = pl.BlockSpec(memory_space=pltpu.SMEM)


def dot(a, b, dims=PLAIN):
    return lax.dot_general(a, b, dims, preferred_element_type=f32)


def split_kernel(heads, size, *refs):
    sources, out_ref, staged, parted, arrived, sent = refs[:4], *refs[4:]
    steps = arrived.shape[1]
    rows = staged.shape[1] // steps

    def fetch(place, step):
        here = pl.ds(step * rows, rows)
        return pltpu.make_async_copy(
            sources[place].at[here], staged.at[place, here], arrived.at[place, step]
        )

    def store(place, step):
        here = pl.ds(step * rows, rows)
        return pltpu.make_async_copy(
            parted.at[:, place, here], out_ref.at[:, place, here], sent.at[place, step]
        )

    for step in range(steps):
        for place in range(4):
            fetch(place, step).start()
    for step in range(steps):
        here = pl.ds(step * rows, rows)
        for place in range(4):
            fetch(place, step).wait()
            for head in range(heads):
                parted[head, place, here] = staged[place, here, head * size : (head + 1) * size]
            store(place, step).start()
    for step in range(steps):
        for place in range(4):
            store(place, step).wait()


def join_kernel(heads, size, *refs):
    source, outs, staged, sent = refs[0], refs[1:5], refs[5], refs[6]
    steps = sent.shape[1]
    rows = staged.shape[1] // steps

    def store(place, step):
        here = pl.ds(step * rows, rows)
        return pltpu.make_async_copy(
            staged.at[place, here], outs[place].at[here], sent.at[place, step]
        )

    for step in range(steps):
        here = pl.ds(step * rows, rows)
        for place in range(4):
            for head in range(heads):
                staged[place, here, head * size : (head + 1) * size] = source[head, place, here]
            store(place, step).start()
    for step in range(steps):
        for place in range(4):
            store(place, step).wait()


def attention_kernel(block_q, length_ref, scale_ref, x_ref, out_ref, term_ref, *scratch):
    tokens = x_ref.shape[0] * x_ref.shape[2]
    length = length_ref[0]
    half = tokens // 2

    @pl.when(length <= half)
    def _():
        attend_keys(half, block_q, length, scale_ref, x_ref, out_ref, term_ref, *scratch)

    @pl.when(length > half)
    def _():
        attend_keys(tokens, block_q, length, scale_ref, x_ref, out_ref, term_ref, *scratch)


def attend_keys(
    width, block_q, length, scale_ref, x_ref, out_ref, term_ref,
    keys_t, values_t, scaled_ref, grads_ref, scores, expos, dprobs, dkeys, dvalues, sent_q, sent_k, results,
):
    blocks, operands, part, size = x_ref.shape
    tokens = blocks * part
    inverse = 1.0 / math.sqrt(size)
    factor = inverse * math.log2(math.e)
    q_blocks = (length + block_q - 1) // block_q
    q_parts, k_parts = block_q // part, width // part
    scale = scale_ref[...]
    rows = pl.ds(0, width)

    def rows_of(block, parts, operand):
        return x_ref[pl.ds(block * parts, parts), operand].reshape(parts * part, size)

    def query_rows(block):
        return pl.ds(pl.multiple_of(block * block_q, block_q), block_q)

    def fold(wide, op):
        return op(op(wide.reshape(width // 8, 8, block_q), axis=0), axis=0, keepdims=True)

    def valid_rows(block):
        return lax.broadcasted_iota(jnp.int32, (block_q, size), 0) + block * block_q < length

    def send_queries(block):
        here = pl.ds(block * q_parts, q_parts)
        return pltpu.make_async_copy(
            results.at[here, 0:2], out_ref.at[here, 0:2], sent_q.at[block]
        )

    def send_keys(block):
        here = pl.ds(block * q_parts, q_parts)
        return pltpu.make_async_copy(
            results.at[here, 2:4], out_ref.at[here, 2:4], sent_k.at[block]
        )

    def prepare_queries(block, carry):
        here = query_rows(block)
        scaled_ref[here, :] = (rows_of(block, q_parts, 0).astype(f32) * scale).astype(bf16)
        grads = rows_of(block, q_parts, 3).astype(f32)
        grads_ref[here, :] = jnp.where(valid_rows(block), grads, 0.0).astype(bf16)
        return carry

    def sweep(third=None, second=None, first=None):
        results_of = ()
        if third:
            block_c, share, delta = third
            scaled_c, grads_c = scaled_ref[query_rows(block_c), :], grads_ref[query_rows(block_c), :]
            probs = expos[rows, :] * share
            probs_b = probs.astype(bf16)
            dscore = (probs * (dprobs[rows, :] - delta)).astype(bf16)
            dvalues[rows, :] += dot(probs_b, grads_c)
            dkeys[rows, :] += dot(dscore, scaled_c)
            results_of += (dot(values_t[:, rows], probs_b), dot(keys_t[:, rows], dscore))
        if second:
            block_b, top = second
            dprob = dot(rows_of(0, k_parts, 2), grads_ref[query_rows(block_b), :], ALONG_ROWS)
            expo = jnp.exp2((scores[rows, :] - top) * factor)
            expos[rows, :] = expo
            dprobs[rows, :] = dprob
            share = 1.0 / fold(expo, jnp.sum)
            results_of += (share, fold(expo * dprob, jnp.sum) * share)
        if first is not None:
            raw = dot(rows_of(0, k_parts, 1), scaled_ref[query_rows(first), :], ALONG_ROWS)
            places = lax.broadcasted_iota(jnp.int32, (width, block_q), 0)
            raw = jnp.where(places < length, raw, NEG)
            scores[rows, :] = raw
            results_of += (fold(raw, jnp.max),)
        return results_of

    def finish_block(block, out_t, dscaled_t):
        attended = jnp.where(valid_rows(block), out_t.T, 0.0).astype(bf16)
        dscaled = (dscaled_t.T * inverse).astype(bf16).astype(f32)
        queries = rows_of(block, q_parts, 0).astype(f32)
        term_ref[...] += jnp.sum((dscaled * queries).reshape(block_q // 8, 8, size), axis=0)
        here = pl.ds(block * q_parts, q_parts)
        results[here, 0] = attended.reshape(q_parts, part, size)
        results[here, 1] = (dscaled * scale).astype(bf16).reshape(q_parts, part, size)
        send_queries(block).start()

    lax.fori_loop(0, q_blocks, prepare_queries, 0)
    last = q_blocks - 1
    (top,) = sweep(first=0)
    for start in range(0, width, 512):
        span = min(512, width - start)
        here = pl.ds(start, span)
        keys_t[:, here] = rows_of(start // span, span // part, 1).T
        values_t[:, here] = rows_of(start // span, span // part, 2).T
    term_ref[...] = jnp.zeros_like(term_ref)
    dkeys[rows, :] = jnp.zeros((width, size), f32)
    dvalues[rows, :] = jnp.zeros((width, size), f32)
    share, delta, top = sweep(second=(0, top), first=jnp.minimum(1, last))

    def query_block(block, carry):
        share, delta, top = carry
        after = jnp.minimum(block + 1, last)
        out_t, dscaled_t, *carry = sweep((block, share, delta), (after, top), jnp.minimum(block + 2, last))
        finish_block(block, out_t, dscaled_t)
        return tuple(carry)

    share, delta, top = lax.fori_loop(0, last, query_block, (share, delta, top))
    finish_block(last, *sweep((last, share, delta)))

    def clear_queries(block, carry):
        results[pl.ds(block * q_parts, q_parts), 0:2] = jnp.zeros((q_parts, 2, part, size), bf16)
        send_queries(block).start()
        return carry

    lax.fori_loop(q_blocks, tokens // block_q, clear_queries, 0)
    for block in range(tokens // block_q):
        here, mine = pl.ds(block * q_parts, q_parts), pl.ds(block * block_q, block_q)
        if block * block_q < width:
            results[here, 2] = (dkeys[mine, :] * inverse).astype(bf16).reshape(q_parts, part, size)
            results[here, 3] = dvalues[mine, :].astype(bf16).reshape(q_parts, part, size)
        else:
            results[here, 2:4] = jnp.zeros((q_parts, 2, part, size), bf16)
        send_keys(block).start()
    for block in range(tokens // block_q):
        send_queries(block).wait()
        send_keys(block).wait()


def attend(length, scale, x):
    blocks, _, part, size = x.shape
    tokens = blocks * part
    block_q = min(BLOCK_Q, tokens)
    copies = tokens // block_q
    return pl.pallas_call(
        functools.partial(attention_kernel, block_q),
        out_shape=(jax.ShapeDtypeStruct(x.shape, bf16), jax.ShapeDtypeStruct((8, size), f32)),
        in_specs=[SMEM, VMEM, VMEM],
        out_specs=(HBM, VMEM),
        scratch_shapes=[pltpu.VMEM((size, tokens), bf16)] * 2
        + [pltpu.VMEM((tokens, size), bf16)] * 2
        + [pltpu.VMEM((tokens, block_q), f32)] * 3
        + [pltpu.VMEM((tokens, size), f32)] * 2
        + [pltpu.SemaphoreType.DMA((copies,))] * 2
        + [pltpu.VMEM(x.shape, bf16)],
        cost_estimate=pl.CostEstimate(
            flops=12 * tokens * tokens * size, bytes_accessed=4 * x.size, transcendentals=tokens * tokens
        ),
        compiler_params=pltpu.CompilerParams(vmem_limit_bytes=48 * 1024 * 1024),
        name="attention",
    )(length, scale, x)


def per_device(queries, keys, values, grads_out, q_scale, lengths):
    heads, size = q_scale.shape
    local, width = queries.shape[1:]
    seq = ("xh", "y")
    me = lax.axis_index(seq)
    small = pltpu.CompilerParams(vmem_limit_bytes=16 * 1024 * 1024)
    steps = max(local // 32, 1)
    x = pl.pallas_call(
        functools.partial(split_kernel, heads, size),
        out_shape=jax.ShapeDtypeStruct((heads, 4, local, size), bf16),
        in_specs=[HBM] * 4,
        out_specs=HBM,
        scratch_shapes=[
            pltpu.VMEM((4, local, width), bf16),
            pltpu.VMEM((heads, 4, local, size), bf16),
            pltpu.SemaphoreType.DMA((4, steps)),
            pltpu.SemaphoreType.DMA((4, steps)),
        ],
        compiler_params=pltpu.CompilerParams(vmem_limit_bytes=56 * 1024 * 1024),
        name="split",
    )(queries[0], keys[0], values[0], grads_out[0])
    x = lax.all_to_all(x, seq, 0, 0, tiled=True)
    scale = lax.dynamic_slice_in_dim(q_scale, me, 1, 0)
    results, term = attend(lengths, scale, x)
    back = lax.all_to_all(results, seq, 0, 0, tiled=True)

    term = jnp.sum(term, axis=0, keepdims=True)
    across = lax.ppermute(term, "xh", [(0, 1), (1, 0)])
    own = lax.broadcasted_iota(jnp.int32, (2, size), 0) == lax.axis_index("xh")
    pair = jnp.where(own, term, across)
    for axis in ("c", "xl", "z"):
        pair = lax.psum(pair, axis)
    grid = lax.all_gather(pair, "y", axis=1).reshape(heads, size)

    outs = pl.pallas_call(
        functools.partial(join_kernel, heads, size),
        out_shape=[jax.ShapeDtypeStruct((local, width), bf16)] * 4,
        in_specs=[VMEM],
        out_specs=[HBM] * 4,
        scratch_shapes=[
            pltpu.VMEM((4, local, width), bf16),
            pltpu.SemaphoreType.DMA((4, steps)),
        ],
        compiler_params=small,
        name="join",
    )(back)
    return tuple(out[None] for out in outs) + (grid,)


def solution(mesh):
    fine = Mesh(mesh.devices.reshape(2, 8, 2, 2, 8), ("xl", "z", "c", "xh", "y"))
    tokens = P(("xl", "z", "c"), ("xh", "y"), None)
    return jax.shard_map(
        per_device,
        mesh=fine,
        in_specs=(tokens, tokens, tokens, tokens, P(), P(("xl", "z", "c"))),
        out_specs=(tokens, tokens, tokens, tokens, P()),
        check_vma=False,
    )
```

```python
import functools
import math

import jax
import jax.numpy as jnp
from jax import lax
from jax.experimental import pallas as pl
from jax.experimental.pallas import tpu as pltpu
from jax.sharding import Mesh, PartitionSpec as P

f32 = jnp.float32
bf16 = jnp.bfloat16
NEG = -1e30
BLOCK_Q = 512
ALONG_ROWS = (((1,), (1,)), ((), ()))
PLAIN = (((1,), (0,)), ((), ()))
VMEM = pl.BlockSpec(memory_space=pltpu.VMEM)
HBM = pl.BlockSpec(memory_space=pltpu.HBM)
SMEM = pl.BlockSpec(memory_space=pltpu.SMEM)


def dot(a, b, dims=PLAIN):
    return lax.dot_general(a, b, dims, preferred_element_type=f32)


def split_kernel(heads, size, *refs):
    sources, out_ref, staged, parted, arrived, sent = refs[:4], *refs[4:]
    steps = arrived.shape[1]
    rows = staged.shape[1] // steps

    def fetch(place, step):
        here = pl.ds(step * rows, rows)
        return pltpu.make_async_copy(
            sources[place].at[here], staged.at[place, here], arrived.at[place, step]
        )

    def store(place, step):
        here = pl.ds(step * rows, rows)
        return pltpu.make_async_copy(
            parted.at[:, place, here], out_ref.at[:, place, here], sent.at[place, step]
        )

    for step in range(steps):
        for place in range(4):
            fetch(place, step).start()
    for step in range(steps):
        here = pl.ds(step * rows, rows)
        for place in range(4):
            fetch(place, step).wait()
            for head in range(heads):
                parted[head, place, here] = staged[place, here, head * size : (head + 1) * size]
            store(place, step).start()
    for step in range(steps):
        for place in range(4):
            store(place, step).wait()


def join_kernel(heads, size, *refs):
    source, outs, staged, sent = refs[0], refs[1:5], refs[5], refs[6]
    steps = sent.shape[1]
    rows = staged.shape[1] // steps

    def store(place, step):
        here = pl.ds(step * rows, rows)
        return pltpu.make_async_copy(
            staged.at[place, here], outs[place].at[here], sent.at[place, step]
        )

    for step in range(steps):
        here = pl.ds(step * rows, rows)
        for place in range(4):
            for head in range(heads):
                staged[place, here, head * size : (head + 1) * size] = source[head, place, here]
            store(place, step).start()
    for step in range(steps):
        for place in range(4):
            store(place, step).wait()


def attention_kernel(block_q, length_ref, scale_ref, x_ref, spent_ref, out_ref, term_ref, *scratch):
    del spent_ref
    tokens = x_ref.shape[0] * x_ref.shape[2]
    length = length_ref[0]
    half = tokens // 2

    @pl.when(length <= half)
    def _():
        attend_keys(half, block_q, length, scale_ref, x_ref, out_ref, term_ref, *scratch)

    @pl.when(length > half)
    def _():
        attend_keys(tokens, block_q, length, scale_ref, x_ref, out_ref, term_ref, *scratch)


def attend_keys(
    width, block_q, length, scale_ref, x_ref, out_ref, term_ref,
    keys_t, values_t, scaled_ref, grads_ref, scores, expos, dprobs, dkeys, dvalues, sent_q, sent_k, results,
):
    blocks, operands, part, size = x_ref.shape
    tokens = blocks * part
    inverse = 1.0 / math.sqrt(size)
    factor = inverse * math.log2(math.e)
    q_blocks = (length + block_q - 1) // block_q
    q_parts, k_parts = block_q // part, width // part
    scale = scale_ref[...]
    rows = pl.ds(0, width)

    def rows_of(block, parts, operand):
        return x_ref[pl.ds(block * parts, parts), operand].reshape(parts * part, size)

    def query_rows(block):
        return pl.ds(pl.multiple_of(block * block_q, block_q), block_q)

    def fold(wide, op):
        return op(op(wide.reshape(width // 8, 8, block_q), axis=0), axis=0, keepdims=True)

    def valid_rows(block):
        return lax.broadcasted_iota(jnp.int32, (block_q, size), 0) + block * block_q < length

    def send_queries(block):
        here = pl.ds(block * q_parts, q_parts)
        return pltpu.make_async_copy(
            results.at[here, 0:2], out_ref.at[here, 0:2], sent_q.at[block]
        )

    def send_keys(block):
        here = pl.ds(block * q_parts, q_parts)
        return pltpu.make_async_copy(
            results.at[here, 2:4], out_ref.at[here, 2:4], sent_k.at[block]
        )

    def prepare_queries(block, carry):
        here = query_rows(block)
        scaled_ref[here, :] = (rows_of(block, q_parts, 0).astype(f32) * scale).astype(bf16)
        grads = rows_of(block, q_parts, 3).astype(f32)
        grads_ref[here, :] = jnp.where(valid_rows(block), grads, 0.0).astype(bf16)
        return carry

    def sweep(third=None, second=None, first=None):
        results_of = ()
        if third:
            block_c, share, delta = third
            scaled_c, grads_c = scaled_ref[query_rows(block_c), :], grads_ref[query_rows(block_c), :]
            probs = expos[rows, :] * share
            probs_b = probs.astype(bf16)
            dscore = (probs * (dprobs[rows, :] - delta)).astype(bf16)
            dvalues[rows, :] += dot(probs_b, grads_c)
            dkeys[rows, :] += dot(dscore, scaled_c)
            results_of += (dot(values_t[:, rows], probs_b), dot(keys_t[:, rows], dscore))
        if second:
            block_b, top = second
            dprob = dot(rows_of(0, k_parts, 2), grads_ref[query_rows(block_b), :], ALONG_ROWS)
            expo = jnp.exp2((scores[rows, :] - top) * factor)
            expos[rows, :] = expo
            dprobs[rows, :] = dprob
            share = 1.0 / fold(expo, jnp.sum)
            results_of += (share, fold(expo * dprob, jnp.sum) * share)
        if first is not None:
            raw = dot(rows_of(0, k_parts, 1), scaled_ref[query_rows(first), :], ALONG_ROWS)
            places = lax.broadcasted_iota(jnp.int32, (width, block_q), 0)
            raw = jnp.where(places < length, raw, NEG)
            scores[rows, :] = raw
            results_of += (fold(raw, jnp.max),)
        return results_of

    def finish_block(block, out_t, dscaled_t):
        attended = jnp.where(valid_rows(block), out_t.T, 0.0).astype(bf16)
        dscaled = (dscaled_t.T * inverse).astype(bf16).astype(f32)
        queries = rows_of(block, q_parts, 0).astype(f32)
        term_ref[...] += jnp.sum((dscaled * queries).reshape(block_q // 8, 8, size), axis=0)
        here = pl.ds(block * q_parts, q_parts)
        results[here, 0] = attended.reshape(q_parts, part, size)
        results[here, 1] = (dscaled * scale).astype(bf16).reshape(q_parts, part, size)
        send_queries(block).start()

    lax.fori_loop(0, q_blocks, prepare_queries, 0)
    last = q_blocks - 1
    (top,) = sweep(first=0)
    for start in range(0, width, 512):
        span = min(512, width - start)
        here = pl.ds(start, span)
        keys_t[:, here] = rows_of(start // span, span // part, 1).T
        values_t[:, here] = rows_of(start // span, span // part, 2).T
    term_ref[...] = jnp.zeros_like(term_ref)
    dkeys[rows, :] = jnp.zeros((width, size), f32)
    dvalues[rows, :] = jnp.zeros((width, size), f32)
    share, delta, top = sweep(second=(0, top), first=jnp.minimum(1, last))

    def query_block(block, carry):
        share, delta, top = carry
        after = jnp.minimum(block + 1, last)
        out_t, dscaled_t, *carry = sweep((block, share, delta), (after, top), jnp.minimum(block + 2, last))
        finish_block(block, out_t, dscaled_t)
        return tuple(carry)

    share, delta, top = lax.fori_loop(0, last, query_block, (share, delta, top))
    finish_block(last, *sweep((last, share, delta)))

    def clear_queries(block, carry):
        results[pl.ds(block * q_parts, q_parts), 0:2] = jnp.zeros((q_parts, 2, part, size), bf16)
        send_queries(block).start()
        return carry

    lax.fori_loop(q_blocks, tokens // block_q, clear_queries, 0)
    for block in range(tokens // block_q):
        here, mine = pl.ds(block * q_parts, q_parts), pl.ds(block * block_q, block_q)
        if block * block_q < width:
            results[here, 2] = (dkeys[mine, :] * inverse).astype(bf16).reshape(q_parts, part, size)
            results[here, 3] = dvalues[mine, :].astype(bf16).reshape(q_parts, part, size)
        else:
            results[here, 2:4] = jnp.zeros((q_parts, 2, part, size), bf16)
        send_keys(block).start()
    for block in range(tokens // block_q):
        send_queries(block).wait()
        send_keys(block).wait()


def attend(length, scale, x, spent):
    blocks, _, part, size = x.shape
    tokens = blocks * part
    block_q = min(BLOCK_Q, tokens)
    copies = tokens // block_q
    return pl.pallas_call(
        functools.partial(attention_kernel, block_q),
        out_shape=(jax.ShapeDtypeStruct(x.shape, bf16), jax.ShapeDtypeStruct((8, size), f32)),
        in_specs=[SMEM, VMEM, VMEM, HBM],
        out_specs=(HBM, VMEM),
        input_output_aliases={3: 0},
        scratch_shapes=[pltpu.VMEM((size, tokens), bf16)] * 2
        + [pltpu.VMEM((tokens, size), bf16)] * 2
        + [pltpu.VMEM((tokens, block_q), f32)] * 3
        + [pltpu.VMEM((tokens, size), f32)] * 2
        + [pltpu.SemaphoreType.DMA((copies,))] * 2
        + [pltpu.VMEM(x.shape, bf16)],
        cost_estimate=pl.CostEstimate(
            flops=12 * tokens * tokens * size, bytes_accessed=4 * x.size, transcendentals=tokens * tokens
        ),
        compiler_params=pltpu.CompilerParams(vmem_limit_bytes=48 * 1024 * 1024),
        name="attention",
    )(length, scale, x, spent)


def per_device(queries, keys, values, grads_out, q_scale, lengths):
    heads, size = q_scale.shape
    local, width = queries.shape[1:]
    seq = ("xh", "y")
    me = lax.axis_index(seq)
    small = pltpu.CompilerParams(vmem_limit_bytes=16 * 1024 * 1024)
    steps = max(local // 32, 1)
    x = pl.pallas_call(
        functools.partial(split_kernel, heads, size),
        out_shape=jax.ShapeDtypeStruct((heads, 4, local, size), bf16),
        in_specs=[HBM] * 4,
        out_specs=HBM,
        scratch_shapes=[
            pltpu.VMEM((4, local, width), bf16),
            pltpu.VMEM((heads, 4, local, size), bf16),
            pltpu.SemaphoreType.DMA((4, steps)),
            pltpu.SemaphoreType.DMA((4, steps)),
        ],
        compiler_params=pltpu.CompilerParams(vmem_limit_bytes=56 * 1024 * 1024),
        name="split",
    )(queries[0], keys[0], values[0], grads_out[0])
    spent = x
    x = lax.all_to_all(x, seq, 0, 0, tiled=True)
    scale = lax.dynamic_slice_in_dim(q_scale, me, 1, 0)
    results, term = attend(lengths, scale, x, spent)
    back = lax.all_to_all(results, seq, 0, 0, tiled=True)

    term = jnp.sum(term, axis=0, keepdims=True)
    across = lax.ppermute(term, "xh", [(0, 1), (1, 0)])
    own = lax.broadcasted_iota(jnp.int32, (2, size), 0) == lax.axis_index("xh")
    pair = jnp.where(own, term, across)
    for axis in ("c", "xl", "z"):
        pair = lax.psum(pair, axis)
    grid = lax.all_gather(pair, "y", axis=1).reshape(heads, size)

    outs = pl.pallas_call(
        functools.partial(join_kernel, heads, size),
        out_shape=[jax.ShapeDtypeStruct((local, width), bf16)] * 4,
        in_specs=[VMEM],
        out_specs=[HBM] * 4,
        scratch_shapes=[
            pltpu.VMEM((4, local, width), bf16),
            pltpu.SemaphoreType.DMA((4, steps)),
        ],
        compiler_params=small,
        name="join",
    )(back)
    return tuple(out[None] for out in outs) + (grid,)


def solution(mesh):
    fine = Mesh(mesh.devices.reshape(2, 8, 2, 2, 8), ("xl", "z", "c", "xh", "y"))
    tokens = P(("xl", "z", "c"), ("xh", "y"), None)
    return jax.shard_map(
        per_device,
        mesh=fine,
        in_specs=(tokens, tokens, tokens, tokens, P(), P(("xl", "z", "c"))),
        out_specs=(tokens, tokens, tokens, tokens, P()),
        check_vma=False,
    )
```

```python
import functools
import math

import jax
import jax.numpy as jnp
from jax import lax
from jax.experimental import pallas as pl
from jax.experimental.pallas import tpu as pltpu
from jax.sharding import Mesh, PartitionSpec as P

f32 = jnp.float32
bf16 = jnp.bfloat16
NEG = -1e30
BLOCK_Q = 512
ALONG_ROWS = (((1,), (1,)), ((), ()))
PLAIN = (((1,), (0,)), ((), ()))
VMEM = pl.BlockSpec(memory_space=pltpu.VMEM)
HBM = pl.BlockSpec(memory_space=pltpu.HBM)
SMEM = pl.BlockSpec(memory_space=pltpu.SMEM)


def dot(a, b, dims=PLAIN):
    return lax.dot_general(a, b, dims, preferred_element_type=f32)


def split_kernel(heads, size, *refs):
    sources, out_ref, staged, parted, arrived, sent = refs[:4], *refs[4:]
    steps = arrived.shape[1]
    rows = staged.shape[1] // steps

    def fetch(place, step):
        here = pl.ds(step * rows, rows)
        return pltpu.make_async_copy(
            sources[place].at[here], staged.at[place, here], arrived.at[place, step]
        )

    def store(place, step):
        here = pl.ds(step * rows, rows)
        return pltpu.make_async_copy(
            parted.at[:, place, here], out_ref.at[:, place, here], sent.at[place, step]
        )

    for step in range(steps):
        for place in range(4):
            fetch(place, step).start()
    for step in range(steps):
        here = pl.ds(step * rows, rows)
        for place in range(4):
            fetch(place, step).wait()
            for head in range(heads):
                parted[head, place, here] = staged[place, here, head * size : (head + 1) * size]
            store(place, step).start()
    for step in range(steps):
        for place in range(4):
            store(place, step).wait()


def join_kernel(heads, size, *refs):
    source, outs, staged, sent = refs[0], refs[1:5], refs[5], refs[6]
    steps = sent.shape[1]
    rows = staged.shape[1] // steps

    def store(place, step):
        here = pl.ds(step * rows, rows)
        return pltpu.make_async_copy(
            staged.at[place, here], outs[place].at[here], sent.at[place, step]
        )

    for step in range(steps):
        here = pl.ds(step * rows, rows)
        for place in range(4):
            for head in range(heads):
                staged[place, here, head * size : (head + 1) * size] = source[head, place, here]
            store(place, step).start()
    for step in range(steps):
        for place in range(4):
            store(place, step).wait()


def attention_kernel(block_q, length_ref, scale_ref, x_ref, spent_ref, out_ref, term_ref, *scratch):
    del spent_ref
    tokens = x_ref.shape[0] * x_ref.shape[2]
    length = length_ref[0]
    half = tokens // 2

    @pl.when(length <= half)
    def _():
        attend_keys(half, block_q, length, scale_ref, x_ref, out_ref, term_ref, *scratch)

    @pl.when(length > half)
    def _():
        attend_keys(tokens, block_q, length, scale_ref, x_ref, out_ref, term_ref, *scratch)


def attend_keys(
    width, block_q, length, scale_ref, x_ref, out_ref, term_ref,
    keys_t, values_t, scaled_ref, grads_ref, scores, expos, dprobs, dkeys, dvalues, sent_q, sent_k, results,
):
    blocks, operands, part, size = x_ref.shape
    tokens = blocks * part
    inverse = 1.0 / math.sqrt(size)
    factor = inverse * math.log2(math.e)
    q_blocks = (length + block_q - 1) // block_q
    q_parts, k_parts = block_q // part, width // part
    scale = scale_ref[...]
    rows = pl.ds(0, width)

    def rows_of(block, parts, operand):
        return x_ref[pl.ds(block * parts, parts), operand].reshape(parts * part, size)

    def query_rows(block):
        return pl.ds(pl.multiple_of(block * block_q, block_q), block_q)

    def fold(wide, op):
        return op(op(wide.reshape(width // 8, 8, block_q), axis=0), axis=0, keepdims=True)

    def valid_rows(block):
        return lax.broadcasted_iota(jnp.int32, (block_q, size), 0) + block * block_q < length

    def send_queries(block):
        here = pl.ds(block * q_parts, q_parts)
        return pltpu.make_async_copy(
            results.at[here, 0:2], out_ref.at[here, 0:2], sent_q.at[block]
        )

    def send_keys(block):
        here = pl.ds(block * q_parts, q_parts)
        return pltpu.make_async_copy(
            results.at[here, 2:4], out_ref.at[here, 2:4], sent_k.at[block]
        )

    def prepare_queries(block, carry):
        here = query_rows(block)
        scaled_ref[here, :] = (rows_of(block, q_parts, 0).astype(f32) * scale).astype(bf16)
        grads = rows_of(block, q_parts, 3).astype(f32)
        grads_ref[here, :] = jnp.where(valid_rows(block), grads, 0.0).astype(bf16)
        return carry

    def sweep(third=None, second=None, first=None):
        results_of = ()
        if third:
            block_c, share, delta = third
            scaled_c, grads_c = scaled_ref[query_rows(block_c), :], grads_ref[query_rows(block_c), :]
            probs = expos[rows, :] * share
            probs_b = probs.astype(bf16)
            dscore = (probs * (dprobs[rows, :] - delta)).astype(bf16)
            dvalues[rows, :] += dot(probs_b, grads_c)
            dkeys[rows, :] += dot(dscore, scaled_c)
            results_of += (dot(values_t[:, rows], probs_b), dot(keys_t[:, rows], dscore))
        if second:
            block_b, top = second
            dprob = dot(rows_of(0, k_parts, 2), grads_ref[query_rows(block_b), :], ALONG_ROWS)
            expo = jnp.exp2((scores[rows, :] - top) * factor)
            expos[rows, :] = expo
            dprobs[rows, :] = dprob
            share = 1.0 / fold(expo, jnp.sum)
            results_of += (share, fold(expo * dprob, jnp.sum) * share)
        if first is not None:
            raw = dot(rows_of(0, k_parts, 1), scaled_ref[query_rows(first), :], ALONG_ROWS)
            places = lax.broadcasted_iota(jnp.int32, (width, block_q), 0)
            raw = jnp.where(places < length, raw, NEG)
            scores[rows, :] = raw
            results_of += (fold(raw, jnp.max),)
        return results_of

    def finish_block(block, out_t, dscaled_t):
        attended = jnp.where(valid_rows(block), out_t.T, 0.0).astype(bf16)
        dscaled = (dscaled_t.T * inverse).astype(bf16).astype(f32)
        queries = rows_of(block, q_parts, 0).astype(f32)
        term_ref[...] += jnp.sum((dscaled * queries).reshape(block_q // 8, 8, size), axis=0)
        here = pl.ds(block * q_parts, q_parts)
        results[here, 0] = attended.reshape(q_parts, part, size)
        results[here, 1] = (dscaled * scale).astype(bf16).reshape(q_parts, part, size)
        send_queries(block).start()

    lax.fori_loop(0, q_blocks, prepare_queries, 0)
    last = q_blocks - 1
    (top,) = sweep(first=0)
    for start in range(0, width, 512):
        span = min(512, width - start)
        here = pl.ds(start, span)
        keys_t[:, here] = rows_of(start // span, span // part, 1).T
        values_t[:, here] = rows_of(start // span, span // part, 2).T
    term_ref[...] = jnp.zeros_like(term_ref)
    dkeys[rows, :] = jnp.zeros((width, size), f32)
    dvalues[rows, :] = jnp.zeros((width, size), f32)
    share, delta, top = sweep(second=(0, top), first=jnp.minimum(1, last))

    def query_block(block, carry):
        share, delta, top = carry
        out_t, dscaled_t, *carry = sweep((block, share, delta), (block + 1, top), block + 2)
        finish_block(block, out_t, dscaled_t)
        return tuple(carry)

    def next_to_last(block, carry):
        share, delta, top = carry
        out_t, dscaled_t, share, delta = sweep((block, share, delta), (block + 1, top))
        finish_block(block, out_t, dscaled_t)
        return share, delta, top

    before = jnp.maximum(last - 1, 0)
    carry = lax.fori_loop(0, before, query_block, (share, delta, top))
    share, delta, top = lax.fori_loop(before, last, next_to_last, carry)
    finish_block(last, *sweep((last, share, delta)))

    def clear_queries(block, carry):
        results[pl.ds(block * q_parts, q_parts), 0:2] = jnp.zeros((q_parts, 2, part, size), bf16)
        send_queries(block).start()
        return carry

    lax.fori_loop(q_blocks, tokens // block_q, clear_queries, 0)
    for block in range(tokens // block_q):
        here, mine = pl.ds(block * q_parts, q_parts), pl.ds(block * block_q, block_q)
        if block * block_q < width:
            results[here, 2] = (dkeys[mine, :] * inverse).astype(bf16).reshape(q_parts, part, size)
            results[here, 3] = dvalues[mine, :].astype(bf16).reshape(q_parts, part, size)
        else:
            results[here, 2:4] = jnp.zeros((q_parts, 2, part, size), bf16)
        send_keys(block).start()
    for block in range(tokens // block_q):
        send_queries(block).wait()
        send_keys(block).wait()


def attend(length, scale, x, spent):
    blocks, _, part, size = x.shape
    tokens = blocks * part
    block_q = min(BLOCK_Q, tokens)
    copies = tokens // block_q
    return pl.pallas_call(
        functools.partial(attention_kernel, block_q),
        out_shape=(jax.ShapeDtypeStruct(x.shape, bf16), jax.ShapeDtypeStruct((8, size), f32)),
        in_specs=[SMEM, VMEM, VMEM, HBM],
        out_specs=(HBM, VMEM),
        input_output_aliases={3: 0},
        scratch_shapes=[pltpu.VMEM((size, tokens), bf16)] * 2
        + [pltpu.VMEM((tokens, size), bf16)] * 2
        + [pltpu.VMEM((tokens, block_q), f32)] * 3
        + [pltpu.VMEM((tokens, size), f32)] * 2
        + [pltpu.SemaphoreType.DMA((copies,))] * 2
        + [pltpu.VMEM(x.shape, bf16)],
        cost_estimate=pl.CostEstimate(
            flops=12 * tokens * tokens * size, bytes_accessed=4 * x.size, transcendentals=tokens * tokens
        ),
        compiler_params=pltpu.CompilerParams(vmem_limit_bytes=48 * 1024 * 1024),
        name="attention",
    )(length, scale, x, spent)


def per_device(queries, keys, values, grads_out, q_scale, lengths):
    heads, size = q_scale.shape
    local, width = queries.shape[1:]
    seq = ("xh", "y")
    me = lax.axis_index(seq)
    small = pltpu.CompilerParams(vmem_limit_bytes=16 * 1024 * 1024)
    steps = max(local // 32, 1)
    x = pl.pallas_call(
        functools.partial(split_kernel, heads, size),
        out_shape=jax.ShapeDtypeStruct((heads, 4, local, size), bf16),
        in_specs=[HBM] * 4,
        out_specs=HBM,
        scratch_shapes=[
            pltpu.VMEM((4, local, width), bf16),
            pltpu.VMEM((heads, 4, local, size), bf16),
            pltpu.SemaphoreType.DMA((4, steps)),
            pltpu.SemaphoreType.DMA((4, steps)),
        ],
        compiler_params=pltpu.CompilerParams(vmem_limit_bytes=56 * 1024 * 1024),
        name="split",
    )(queries[0], keys[0], values[0], grads_out[0])
    spent = x
    x = lax.all_to_all(x, seq, 0, 0, tiled=True)
    scale = lax.dynamic_slice_in_dim(q_scale, me, 1, 0)
    results, term = attend(lengths, scale, x, spent)
    back = lax.all_to_all(results, seq, 0, 0, tiled=True)

    term = jnp.sum(term, axis=0, keepdims=True)
    across = lax.ppermute(term, "xh", [(0, 1), (1, 0)])
    own = lax.broadcasted_iota(jnp.int32, (2, size), 0) == lax.axis_index("xh")
    pair = jnp.where(own, term, across)
    for axis in ("c", "xl", "z"):
        pair = lax.psum(pair, axis)
    grid = lax.all_gather(pair, "y", axis=1).reshape(heads, size)

    outs = pl.pallas_call(
        functools.partial(join_kernel, heads, size),
        out_shape=[jax.ShapeDtypeStruct((local, width), bf16)] * 4,
        in_specs=[VMEM],
        out_specs=[HBM] * 4,
        scratch_shapes=[
            pltpu.VMEM((4, local, width), bf16),
            pltpu.SemaphoreType.DMA((4, steps)),
        ],
        compiler_params=small,
        name="join",
    )(back)
    return tuple(out[None] for out in outs) + (grid,)


def solution(mesh):
    fine = Mesh(mesh.devices.reshape(2, 8, 2, 2, 8), ("xl", "z", "c", "xh", "y"))
    tokens = P(("xl", "z", "c"), ("xh", "y"), None)
    return jax.shard_map(
        per_device,
        mesh=fine,
        in_specs=(tokens, tokens, tokens, tokens, P(), P(("xl", "z", "c"))),
        out_specs=(tokens, tokens, tokens, tokens, P()),
        check_vma=False,
    )
```
